768 devices in a mesh: row: 32 (over z_hi, y), col: 6 (over z_lo, core), depth: 4 (over x).
Axes of the slice: x: 4, y: 8, z: 12 (z_hi: 4, z_lo: 3; z = z_hi * 3 + z_lo), core: 2. Of those that a mesh axis runs over, the one named last changes fastest.
Arguments:
- amplitudes: bfloat16 [192, 1536, 2048], P('row', 'col', 'depth'), may hold values from -6 to 6
- integrals: bfloat16 [2048, 2048], replicated, may hold values from -0.375 to 0.375
- pair_irreps: int32 [2048], replicated, may hold values from 0 to 7
- occ_fock: bfloat16 [192, 192], replicated, may hold values from -0.4375 to 0.4375
Outputs:
- residual: bfloat16 [192, 1536, 2048], P('row', 'col', 'depth')
The draws below stay inside these ranges and needn't reach their ends.
All inputs are finite; a program needn't handle non-finite values.
Results may differ from the reference program's by a relative error of at most 0.0039.
Values may be sent and summed in bfloat16 or wider, within the bound.
No kernel may reach another device: no remote copies, remote signals or barrier semaphores. Data moves between devices by JAX's collectives and lax.ppermute only.
A program may use at most 64 MiB of HBM per device.

```python
import jax
import jax.numpy as jnp

W = 2048
IRREPS = 8
IW = 192
JW = 1536


def place_ends(entries, own_key, smallest, top_value):
    place = [jax.random.randint(jax.random.fold_in(own_key, axis), (), 0, length) for axis, length in enumerate(entries.shape)]
    longest = entries.shape.index(max(entries.shape))
    next_to = place[:longest] + [(place[longest] + 1) % entries.shape[longest]] + place[longest + 1:]
    return entries.at[tuple(place)].set(smallest).at[tuple(next_to)].set(top_value)


def shard_levels(key, extent, split, least, top_value):
    factor_of, own = 1.0, jax.random.fold_in(key, 6)
    for dim, shards_of in split:
        heights = jnp.exp(jax.random.uniform(jax.random.fold_in(own, dim), (shards_of,), jnp.float32, least / len(split), top_value / len(split)))
        factor_of = factor_of * jnp.repeat(heights, extent[dim] // shards_of).reshape([-1 if axis == dim else 1 for axis in range(len(extent))])
    return factor_of


def gaussian(stream_key, extent, scale, reach, cuts=(), kind=jnp.bfloat16):
    entries = jax.random.normal(stream_key, extent, jnp.float32) * scale
    if len(cuts) > 0:
        entries = shard_levels(stream_key, extent, cuts, -0.22, 0.18) * entries
    return jnp.clip(entries, min=-reach, max=reach).astype(kind)


def setup_inputs(seed: int = 0) -> dict:
    arg_keys = jax.random.split(jax.random.key(seed), 5)
    amplitudes = gaussian(arg_keys[0], (IW, JW, W), 1.0, 6.0, ((0, 32), (1, 6), (2, 4)))
    integrals = gaussian(arg_keys[1], (W, W), (W // IRREPS) ** -0.5, 0.375)
    pair_irreps = place_ends(jax.random.randint(arg_keys[2], (W,), 0, IRREPS), jax.random.fold_in(arg_keys[2], 1), 0, IRREPS - 1).astype(jnp.int32)
    occ_fock = gaussian(arg_keys[3], (IW, IW), IW ** -0.5, 0.4375)
    return dict(amplitudes=amplitudes, integrals=integrals, pair_irreps=pair_irreps, occ_fock=occ_fock)


def reference(amplitudes, integrals, pair_irreps, occ_fock):
    same = pair_irreps[:, None] == pair_irreps[None, :]
    masked = jnp.where(same, integrals, jnp.zeros_like(integrals))
    flat = amplitudes.reshape(-1, W)
    ladder = jnp.dot(flat, masked, preferred_element_type=jnp.float32).reshape(amplitudes.shape)
    dressed = (-jnp.einsum("ik,kjn->ijn", occ_fock.astype(jnp.float32), amplitudes.astype(jnp.float32))).astype(jnp.bfloat16)
    return (ladder + dressed.astype(jnp.float32)).astype(jnp.bfloat16)
```

```python
import jax
import jax.numpy as jnp
from jax import lax
from jax.experimental import pallas as pl
from jax.experimental.pallas import tpu as pltpu
from jax.sharding import PartitionSpec as P


def ladder_kernel(parts_ref, masked_ref, out_ref):
    depth = parts_ref.shape[0]
    total = jnp.dot(parts_ref[0], masked_ref[0], preferred_element_type=jnp.float32)
    for d in range(1, depth):
        total += jnp.dot(parts_ref[d], masked_ref[d], preferred_element_type=jnp.float32)
    out_ref[...] = total


def ladder_product(parts, masked):
    depth, rows, share = parts.shape
    columns = masked.shape[2]
    steps = 6
    block = rows // steps
    return pl.pallas_call(
        ladder_kernel,
        grid=(steps,),
        in_specs=[
            pl.BlockSpec((depth, block, share), lambda r: (0, r, 0)),
            pl.BlockSpec((depth, share, columns), lambda r: (0, 0, 0)),
        ],
        out_specs=pl.BlockSpec((block, columns), lambda r: (r, 0)),
        out_shape=jax.ShapeDtypeStruct((rows, columns), jnp.float32),
        compiler_params=pltpu.CompilerParams(vmem_limit_bytes=24 * 1024 * 1024),
        cost_estimate=pl.CostEstimate(
            flops=2 * depth * rows * share * columns,
            bytes_accessed=2 * depth * share * (rows + columns) + 4 * rows * columns,
            transcendentals=0,
        ),
        name="ladder",
    )(parts, masked)


def on_device(amplitudes, integrals, pair_irreps, occ_fock):
    local_i, local_j, share = amplitudes.shape
    whole_pairs = integrals.shape[0]
    whole_i = occ_fock.shape[0]
    rows = whole_i // local_i
    depth = whole_pairs // share
    hub_j = local_j // rows
    offset = lax.axis_index("depth") * share

    gathered = lax.all_gather(amplitudes, "depth", axis=0, tiled=False)

    blocks = amplitudes.reshape(local_i, rows, hub_j, share).transpose(1, 0, 2, 3)
    arrived = lax.all_to_all(blocks, "row", split_axis=0, concat_axis=0)
    product = jnp.einsum(
        "ik,kmn->imn",
        occ_fock,
        arrived.reshape(whole_i, hub_j, share),
        preferred_element_type=jnp.float32,
    )
    dressed_part = (-product).astype(jnp.bfloat16).reshape(rows, local_i, hub_j, share)
    dressed = lax.all_to_all(dressed_part, "row", split_axis=0, concat_axis=0)
    dressed = dressed.transpose(1, 0, 2, 3).reshape(local_i, local_j, share)

    own_columns = lax.dynamic_slice(integrals, (0, offset), (whole_pairs, share))
    own_labels = lax.dynamic_slice_in_dim(pair_irreps, offset, share, 0)
    same = pair_irreps[:, None] == own_labels[None, :]
    masked = jnp.where(same, own_columns, jnp.zeros_like(own_columns))
    ladder = ladder_product(
        gathered.reshape(depth, local_i * local_j, share), masked.reshape(depth, share, share)
    ).reshape(local_i, local_j, share)
    return (ladder + dressed.astype(jnp.float32)).astype(jnp.bfloat16)


def solution(mesh):
    placed = (P("row", "col", "depth"), P(), P(), P())
    return jax.shard_map(
        on_device, mesh=mesh, in_specs=placed, out_specs=P("row", "col", "depth"), check_vma=False
    )
```

```python
import jax
import jax.numpy as jnp
from jax import lax
from jax.experimental import pallas as pl
from jax.experimental.pallas import tpu as pltpu
from jax.sharding import PartitionSpec as P


def ladder_kernel(order_ref, *refs):
    part_refs, masked_ref, out_ref = refs[:-2], refs[-2], refs[-1]
    total = None
    for d, part_ref in enumerate(part_refs):
        term = jnp.dot(part_ref[...], masked_ref[order_ref[d]], preferred_element_type=jnp.float32)
        total = term if total is None else total + term
    out_ref[...] = total


def ladder_product(order, parts, masked):
    depth = len(parts)
    rows, share = parts[0].shape
    columns = masked.shape[2]
    steps = 6
    block = rows // steps
    return pl.pallas_call(
        ladder_kernel,
        grid_spec=pltpu.PrefetchScalarGridSpec(
            num_scalar_prefetch=1,
            grid=(steps,),
            in_specs=[pl.BlockSpec((block, share), lambda r, order: (r, 0))] * depth
            + [pl.BlockSpec((depth, share, columns), lambda r, order: (0, 0, 0))],
            out_specs=pl.BlockSpec((block, columns), lambda r, order: (r, 0)),
        ),
        out_shape=jax.ShapeDtypeStruct((rows, columns), jnp.float32),
        compiler_params=pltpu.CompilerParams(vmem_limit_bytes=24 * 1024 * 1024),
        cost_estimate=pl.CostEstimate(
            flops=2 * depth * rows * share * columns,
            bytes_accessed=2 * depth * share * (rows + columns) + 4 * rows * columns,
            transcendentals=0,
        ),
        name="ladder",
    )(order, *parts, masked)


def on_device(amplitudes, integrals, pair_irreps, occ_fock):
    local_i, local_j, share = amplitudes.shape
    whole_pairs = integrals.shape[0]
    whole_i = occ_fock.shape[0]
    rows = whole_i // local_i
    depth = whole_pairs // share
    hub_j = local_j // rows
    offset = lax.axis_index("depth") * share

    parts = [amplitudes] + [
        lax.ppermute(amplitudes, "depth", [(d, (d + step) % depth) for d in range(depth)])
        for step in range(1, depth)
    ]
    order = (lax.axis_index("depth") - jnp.arange(depth, dtype=jnp.int32) + depth) % depth

    blocks = amplitudes.reshape(local_i, rows, hub_j, share).transpose(1, 0, 2, 3)
    arrived = lax.all_to_all(blocks, "row", split_axis=0, concat_axis=0)
    product = jnp.einsum(
        "ik,kmn->imn",
        occ_fock,
        arrived.reshape(whole_i, hub_j, share),
        preferred_element_type=jnp.float32,
    )
    dressed_part = (-product).astype(jnp.bfloat16).reshape(rows, local_i, hub_j, share)
    dressed = lax.all_to_all(dressed_part, "row", split_axis=0, concat_axis=0)
    dressed = dressed.transpose(1, 0, 2, 3).reshape(local_i, local_j, share)

    own_columns = lax.dynamic_slice(integrals, (0, offset), (whole_pairs, share))
    own_labels = lax.dynamic_slice_in_dim(pair_irreps, offset, share, 0)
    same = pair_irreps[:, None] == own_labels[None, :]
    masked = jnp.where(same, own_columns, jnp.zeros_like(own_columns))
    ladder = ladder_product(
        order,
        [part.reshape(local_i * local_j, share) for part in parts],
        masked.reshape(depth, share, share),
    ).reshape(local_i, local_j, share)
    return (ladder + dressed.astype(jnp.float32)).astype(jnp.bfloat16)


def solution(mesh):
    placed = (P("row", "col", "depth"), P(), P(), P())
    return jax.shard_map(
        on_device, mesh=mesh, in_specs=placed, out_specs=P("row", "col", "depth"), check_vma=False
    )
```

```python
import jax
import jax.numpy as jnp
from jax import lax
from jax.experimental import pallas as pl
from jax.experimental.pallas import tpu as pltpu
from jax.sharding import PartitionSpec as P


def ladder_kernel(order_ref, own_ref, below_ref, above_ref, far_low_ref, far_high_ref, masked_ref, out_ref):
    low = pl.program_id(0) < pl.num_programs(0) // 2
    far = jnp.where(low, far_low_ref[...], far_high_ref[...])
    total = jnp.dot(own_ref[...], masked_ref[order_ref[0]], preferred_element_type=jnp.float32)
    total += jnp.dot(below_ref[...], masked_ref[order_ref[1]], preferred_element_type=jnp.float32)
    total += jnp.dot(above_ref[...], masked_ref[order_ref[3]], preferred_element_type=jnp.float32)
    total += jnp.dot(far, masked_ref[order_ref[2]], preferred_element_type=jnp.float32)
    out_ref[...] = total


def ladder_product(order, own, below, above, far_low, far_high, masked):
    depth, share, columns = masked.shape
    rows = own.shape[0]
    steps = 6
    half = steps // 2
    block = rows // steps
    whole = pl.BlockSpec((block, share), lambda r, order: (r, 0))
    return pl.pallas_call(
        ladder_kernel,
        grid_spec=pltpu.PrefetchScalarGridSpec(
            num_scalar_prefetch=1,
            grid=(steps,),
            in_specs=[
                whole,
                whole,
                whole,
                pl.BlockSpec((block, share), lambda r, order: (jnp.minimum(r, half - 1), 0)),
                pl.BlockSpec((block, share), lambda r, order: (jnp.maximum(r - half, 0), 0)),
                pl.BlockSpec((depth, share, columns), lambda r, order: (0, 0, 0)),
            ],
            out_specs=pl.BlockSpec((block, columns), lambda r, order: (r, 0)),
        ),
        out_shape=jax.ShapeDtypeStruct((rows, columns), jnp.float32),
        compiler_params=pltpu.CompilerParams(vmem_limit_bytes=24 * 1024 * 1024),
        cost_estimate=pl.CostEstimate(
            flops=2 * depth * rows * share * columns,
            bytes_accessed=2 * depth * share * (rows + columns) + 4 * rows * columns,
            transcendentals=0,
        ),
        name="ladder",
    )(order, own, below, above, far_low, far_high, masked)


def shift(block, depth, step):
    return lax.ppermute(block, "depth", [(d, (d + step) % depth) for d in range(depth)])


def on_device(amplitudes, integrals, pair_irreps, occ_fock):
    local_i, local_j, share = amplitudes.shape
    whole_pairs = integrals.shape[0]
    whole_i = occ_fock.shape[0]
    rows = whole_i // local_i
    depth = whole_pairs // share
    hub_j = local_j // rows
    offset = lax.axis_index("depth") * share

    below = shift(amplitudes, depth, 1)
    above = shift(amplitudes, depth, -1)
    order = (lax.axis_index("depth") - jnp.arange(depth, dtype=jnp.int32) + depth) % depth

    blocks = amplitudes.reshape(local_i, rows, hub_j, share).transpose(1, 0, 2, 3)
    arrived = lax.all_to_all(blocks, "row", split_axis=0, concat_axis=0)
    arrived, below, above = lax.optimization_barrier((arrived, below, above))
    far_low = shift(below[: local_i // 2], depth, 1)
    far_high = shift(above[local_i // 2 :], depth, -1)
    product = jnp.einsum(
        "ik,kmn->imn",
        occ_fock,
        arrived.reshape(whole_i, hub_j, share),
        preferred_element_type=jnp.float32,
    )
    dressed_part = (-product).astype(jnp.bfloat16).reshape(rows, local_i, hub_j, share)
    dressed = lax.all_to_all(dressed_part, "row", split_axis=0, concat_axis=0)
    dressed = dressed.transpose(1, 0, 2, 3).reshape(local_i, local_j, share)

    own_columns = lax.dynamic_slice(integrals, (0, offset), (whole_pairs, share))
    own_labels = lax.dynamic_slice_in_dim(pair_irreps, offset, share, 0)
    same = pair_irreps[:, None] == own_labels[None, :]
    masked = jnp.where(same, own_columns, jnp.zeros_like(own_columns))
    ladder = ladder_product(
        order,
        *(part.reshape(-1, share) for part in (amplitudes, below, above, far_low, far_high)),
        masked.reshape(depth, share, share),
    ).reshape(local_i, local_j, share)
    return (ladder + dressed.astype(jnp.float32)).astype(jnp.bfloat16)


def solution(mesh):
    placed = (P("row", "col", "depth"), P(), P(), P())
    return jax.shard_map(
        on_device, mesh=mesh, in_specs=placed, out_specs=P("row", "col", "depth"), check_vma=False
    )
```

```python
import jax
import jax.numpy as jnp
from jax import lax
from jax.experimental import pallas as pl
from jax.experimental.pallas import tpu as pltpu
from jax.sharding import PartitionSpec as P


def ladder_kernel(order_ref, own_ref, below_ref, above_ref, far_low_ref, far_high_ref, masked_ref, out_ref):
    low = pl.program_id(0) < pl.num_programs(0) // 2
    far = jnp.where(low, far_low_ref[...], far_high_ref[...])
    total = jnp.dot(own_ref[...], masked_ref[order_ref[0]], preferred_element_type=jnp.float32)
    total += jnp.dot(below_ref[...], masked_ref[order_ref[1]], preferred_element_type=jnp.float32)
    total += jnp.dot(above_ref[...], masked_ref[order_ref[3]], preferred_element_type=jnp.float32)
    total += jnp.dot(far, masked_ref[order_ref[2]], preferred_element_type=jnp.float32)
    out_ref[...] = total


def ladder_product(order, own, below, above, far_low, far_high, masked):
    depth, share, columns = masked.shape
    rows = own.shape[0]
    steps = 6
    half = steps // 2
    block = rows // steps
    whole = pl.BlockSpec((block, share), lambda r, order: (r, 0))
    return pl.pallas_call(
        ladder_kernel,
        grid_spec=pltpu.PrefetchScalarGridSpec(
            num_scalar_prefetch=1,
            grid=(steps,),
            in_specs=[
                whole,
                whole,
                whole,
                pl.BlockSpec((block, share), lambda r, order: (jnp.minimum(r, half - 1), 0)),
                pl.BlockSpec((block, share), lambda r, order: (jnp.maximum(r - half, 0), 0)),
                pl.BlockSpec((depth, share, columns), lambda r, order: (0, 0, 0)),
            ],
            out_specs=pl.BlockSpec((block, columns), lambda r, order: (r, 0)),
        ),
        out_shape=jax.ShapeDtypeStruct((rows, columns), jnp.float32),
        compiler_params=pltpu.CompilerParams(vmem_limit_bytes=24 * 1024 * 1024),
        cost_estimate=pl.CostEstimate(
            flops=2 * depth * rows * share * columns,
            bytes_accessed=2 * depth * share * (rows + columns) + 4 * rows * columns,
            transcendentals=0,
        ),
        name="ladder",
    )(order, own, below, above, far_low, far_high, masked)


def spread_fock(occ_fock, copies):
    size = occ_fock.shape[0]
    spread = size * copies
    wide = lax.broadcasted_iota(jnp.int32, (spread, size), 0) // copies
    narrow = lax.broadcasted_iota(jnp.int32, (spread, size), 1)
    expand = (wide == narrow).astype(jnp.bfloat16)
    tall = jnp.dot(expand, -occ_fock, preferred_element_type=jnp.float32).astype(jnp.bfloat16)
    full = jnp.dot(tall, expand.T, preferred_element_type=jnp.float32).astype(jnp.bfloat16)
    row = lax.broadcasted_iota(jnp.int32, (spread, spread), 0) % copies
    column = lax.broadcasted_iota(jnp.int32, (spread, spread), 1) % copies
    return jnp.where(row == column, full, jnp.zeros_like(full))


def add_kernel(ladder_ref, dressed_ref, out_ref):
    dressed = dressed_ref[...].astype(jnp.float32).reshape(ladder_ref.shape)
    out_ref[...] = (ladder_ref[...] + dressed).astype(out_ref.dtype)


def add_dressed(ladder, dressed):
    local_i, local_j, share = ladder.shape
    rows, _, hub_j, _ = dressed.shape
    whole = pl.BlockSpec((1, local_j, share), lambda i: (i, 0, 0))
    return pl.pallas_call(
        add_kernel,
        grid=(local_i,),
        in_specs=[whole, pl.BlockSpec((rows, 1, hub_j, share), lambda i: (0, i, 0, 0))],
        out_specs=whole,
        out_shape=jax.ShapeDtypeStruct(ladder.shape, jnp.bfloat16),
        compiler_params=pltpu.CompilerParams(vmem_limit_bytes=16 * 1024 * 1024),
        name="add_dressed",
    )(ladder, dressed)


def shift(block, depth, step):
    return lax.ppermute(block, "depth", [(d, (d + step) % depth) for d in range(depth)])


def on_device(amplitudes, integrals, pair_irreps, occ_fock):
    local_i, local_j, share = amplitudes.shape
    whole_pairs = integrals.shape[0]
    whole_i = occ_fock.shape[0]
    rows = whole_i // local_i
    depth = whole_pairs // share
    hub_j = local_j // rows
    offset = lax.axis_index("depth") * share

    below = shift(amplitudes, depth, 1)
    above = shift(amplitudes, depth, -1)
    order = (lax.axis_index("depth") - jnp.arange(depth, dtype=jnp.int32) + depth) % depth

    blocks = amplitudes.reshape(local_i, rows, hub_j, share).transpose(1, 0, 2, 3)
    arrived = lax.all_to_all(blocks, "row", split_axis=0, concat_axis=0)
    spread = spread_fock(occ_fock, hub_j)
    arrived, below, above, spread = lax.optimization_barrier((arrived, below, above, spread))
    far_low = shift(below[: local_i // 2], depth, 1)
    far_high = shift(above[local_i // 2 :], depth, -1)
    product = jnp.dot(
        spread,
        arrived.reshape(whole_i * hub_j, share),
        preferred_element_type=jnp.float32,
    )
    dressed_part = product.astype(jnp.bfloat16).reshape(rows, local_i, hub_j, share)
    dressed = lax.all_to_all(dressed_part, "row", split_axis=0, concat_axis=0)

    own_columns = lax.dynamic_slice(integrals, (0, offset), (whole_pairs, share))
    own_labels = lax.dynamic_slice_in_dim(pair_irreps, offset, share, 0)
    same = pair_irreps[:, None] == own_labels[None, :]
    masked = jnp.where(same, own_columns, jnp.zeros_like(own_columns))
    ladder = ladder_product(
        order,
        *(part.reshape(-1, share) for part in (amplitudes, below, above, far_low, far_high)),
        masked.reshape(depth, share, share),
    ).reshape(local_i, local_j, share)
    return add_dressed(ladder, dressed)


def solution(mesh):
    placed = (P("row", "col", "depth"), P(), P(), P())
    return jax.shard_map(
        on_device, mesh=mesh, in_specs=placed, out_specs=P("row", "col", "depth"), check_vma=False
    )
```

```python
import jax
import jax.numpy as jnp
from jax import lax
from jax.experimental import pallas as pl
from jax.experimental.pallas import tpu as pltpu
from jax.sharding import PartitionSpec as P


def ladder_kernel(order_ref, own_ref, below_ref, above_ref, far_low_ref, far_high_ref, masked_ref, out_ref):
    low = pl.program_id(0) < pl.num_programs(0) // 2
    far = jnp.where(low, far_low_ref[...], far_high_ref[...])
    total = jnp.dot(own_ref[...], masked_ref[order_ref[0]], preferred_element_type=jnp.float32)
    total += jnp.dot(below_ref[...], masked_ref[order_ref[1]], preferred_element_type=jnp.float32)
    total += jnp.dot(above_ref[...], masked_ref[order_ref[3]], preferred_element_type=jnp.float32)
    total += jnp.dot(far, masked_ref[order_ref[2]], preferred_element_type=jnp.float32)
    out_ref[...] = total


def ladder_product(order, own, below, above, far_low, far_high, masked):
    depth, share, columns = masked.shape
    rows = own.shape[0]
    steps = 6
    half = steps // 2
    block = rows // steps
    whole = pl.BlockSpec((block, share), lambda r, order: (r, 0))
    return pl.pallas_call(
        ladder_kernel,
        grid_spec=pltpu.PrefetchScalarGridSpec(
            num_scalar_prefetch=1,
            grid=(steps,),
            in_specs=[
                whole,
                whole,
                whole,
                pl.BlockSpec((block, share), lambda r, order: (jnp.minimum(r, half - 1), 0)),
                pl.BlockSpec((block, share), lambda r, order: (jnp.maximum(r - half, 0), 0)),
                pl.BlockSpec((depth, share, columns), lambda r, order: (0, 0, 0)),
            ],
            out_specs=pl.BlockSpec((block, columns), lambda r, order: (r, 0)),
        ),
        out_shape=jax.ShapeDtypeStruct((rows, columns), jnp.float32),
        compiler_params=pltpu.CompilerParams(vmem_limit_bytes=24 * 1024 * 1024),
        cost_estimate=pl.CostEstimate(
            flops=2 * depth * rows * share * columns,
            bytes_accessed=2 * depth * share * (rows + columns) + 4 * rows * columns,
            transcendentals=0,
        ),
        name="ladder",
    )(order, own, below, above, far_low, far_high, masked)


def shift(block, depth, step):
    return lax.ppermute(block, "depth", [(d, (d + step) % depth) for d in range(depth)])


def on_device(amplitudes, integrals, pair_irreps, occ_fock):
    local_i, local_j, share = amplitudes.shape
    whole_pairs = integrals.shape[0]
    whole_i = occ_fock.shape[0]
    rows = whole_i // local_i
    depth = whole_pairs // share
    hub_j = local_j // rows
    offset = lax.axis_index("depth") * share

    below = shift(amplitudes, depth, 1)
    above = shift(amplitudes, depth, -1)
    order = (lax.axis_index("depth") - jnp.arange(depth, dtype=jnp.int32) + depth) % depth

    blocks = amplitudes.reshape(local_i, rows, hub_j, share).transpose(1, 0, 2, 3)
    arrived = lax.all_to_all(blocks, "row", split_axis=0, concat_axis=0)
    far_low = shift(below[: local_i // 2], depth, 1)
    far_high = shift(above[local_i // 2 :], depth, -1)
    own_columns = lax.dynamic_slice(integrals, (0, offset), (whole_pairs, share))
    own_labels = lax.dynamic_slice_in_dim(pair_irreps, offset, share, 0)
    same = pair_irreps[:, None] == own_labels[None, :]
    masked = jnp.where(same, own_columns, jnp.zeros_like(own_columns))
    ladder = ladder_product(
        order,
        *(part.reshape(-1, share) for part in (amplitudes, below, above, far_low, far_high)),
        masked.reshape(depth, share, share),
    ).reshape(local_i, local_j, share)
    tied_fock, ladder = lax.optimization_barrier((occ_fock, ladder))
    product = jnp.einsum(
        "ik,kmn->imn",
        tied_fock,
        arrived.reshape(whole_i, hub_j, share),
        preferred_element_type=jnp.float32,
    )
    dressed_part = (-product).astype(jnp.bfloat16).reshape(rows, local_i, hub_j, share)
    dressed = lax.all_to_all(dressed_part, "row", split_axis=0, concat_axis=0)
    dressed = dressed.transpose(1, 0, 2, 3).reshape(local_i, local_j, share)
    return (ladder + dressed.astype(jnp.float32)).astype(jnp.bfloat16)


def solution(mesh):
    placed = (P("row", "col", "depth"), P(), P(), P())
    return jax.shard_map(
        on_device, mesh=mesh, in_specs=placed, out_specs=P("row", "col", "depth"), check_vma=False
    )
```

```python
import jax
import jax.numpy as jnp
from jax import lax
from jax.experimental import pallas as pl
from jax.experimental.pallas import tpu as pltpu
from jax.sharding import PartitionSpec as P


def ladder_kernel(from_ref, to_ref, *refs):
    part_refs, masked_ref, out_ref = refs[:-2], refs[-2], refs[-1]
    share = part_refs[0].shape[1]
    total = None
    for s, part_ref in enumerate(part_refs):
        start = pl.multiple_of(from_ref[s] * share, share)
        term = jnp.dot(
            part_ref[...], masked_ref[pl.ds(start, share), :], preferred_element_type=jnp.float32
        )
        total = term if total is None else total + term
    out_ref[0] = total.astype(out_ref.dtype)


def ladder_product(came_from, goes_to, parts, masked):
    depth = len(parts)
    rows, share = parts[0].shape
    whole_pairs = masked.shape[0]
    return pl.pallas_call(
        ladder_kernel,
        grid_spec=pltpu.PrefetchScalarGridSpec(
            num_scalar_prefetch=2,
            grid=(depth,),
            in_specs=[pl.BlockSpec((rows, share), lambda t, came, goes: (0, 0))] * depth
            + [pl.BlockSpec((whole_pairs, share), lambda t, came, goes: (0, goes[t]))],
            out_specs=pl.BlockSpec((1, rows, share), lambda t, came, goes: (t, 0, 0)),
        ),
        out_shape=jax.ShapeDtypeStruct((depth, rows, share), jnp.bfloat16),
        compiler_params=pltpu.CompilerParams(vmem_limit_bytes=24 * 1024 * 1024),
        cost_estimate=pl.CostEstimate(
            flops=2 * rows * whole_pairs * whole_pairs,
            bytes_accessed=2 * whole_pairs * whole_pairs + 4 * depth * rows * share,
            transcendentals=0,
        ),
        name="ladder",
    )(came_from, goes_to, *parts, masked)


def shift(block, depth, step):
    return lax.ppermute(block, "depth", [(d, (d + step) % depth) for d in range(depth)])


def on_device(amplitudes, integrals, pair_irreps, occ_fock):
    local_i, local_j, share = amplitudes.shape
    whole_pairs = integrals.shape[0]
    whole_i = occ_fock.shape[0]
    rows = whole_i // local_i
    depth = whole_pairs // share
    hub_j = local_j // rows
    part_j = local_j // depth
    here = lax.axis_index("depth")
    steps = jnp.arange(depth, dtype=jnp.int32)
    came_from = (here - steps + depth) % depth
    goes_to = (here + steps) % depth

    blocks = amplitudes.reshape(local_i, rows, hub_j, share).transpose(1, 0, 2, 3)
    arrived = lax.all_to_all(blocks, "row", split_axis=0, concat_axis=0)

    parts = []
    for s in range(depth):
        start = ((here + s) % depth) * part_j
        part = lax.dynamic_slice(amplitudes, (0, start, 0), (local_i, part_j, share))
        parts.append(part if s == 0 else shift(part, depth, s))
    same = pair_irreps[:, None] == pair_irreps[None, :]
    masked = jnp.where(same, integrals, jnp.zeros_like(integrals))
    columns = ladder_product(
        came_from, goes_to, [part.reshape(local_i * part_j, share) for part in parts], masked
    ).reshape(depth, local_i, part_j, share)
    ladder = jnp.zeros_like(amplitudes)
    for t in range(depth):
        piece = columns[0] if t == 0 else shift(columns[t], depth, t)
        start = ((here - t + depth) % depth) * part_j
        ladder = lax.dynamic_update_slice(ladder, piece, (0, start, 0))

    tied_fock, ladder = lax.optimization_barrier((occ_fock, ladder))
    product = jnp.einsum(
        "ik,kmn->imn",
        tied_fock,
        arrived.reshape(whole_i, hub_j, share),
        preferred_element_type=jnp.float32,
    )
    dressed_part = (-product).astype(jnp.bfloat16).reshape(rows, local_i, hub_j, share)
    dressed = lax.all_to_all(dressed_part, "row", split_axis=0, concat_axis=0)
    dressed = dressed.transpose(1, 0, 2, 3).reshape(local_i, local_j, share)
    return (ladder.astype(jnp.float32) + dressed.astype(jnp.float32)).astype(jnp.bfloat16)


def solution(mesh):
    placed = (P("row", "col", "depth"), P(), P(), P())
    return jax.shard_map(
        on_device, mesh=mesh, in_specs=placed, out_specs=P("row", "col", "depth"), check_vma=False
    )
```

```python
import functools

import jax
import jax.numpy as jnp
from jax import lax
from jax.experimental import pallas as pl
from jax.experimental.pallas import tpu as pltpu
from jax.sharding import PartitionSpec as P


def ladder_kernel(depth, from_ref, to_ref, *refs):
    part_refs, masked_ref, out_refs = refs[:depth], refs[depth], refs[depth + 1 :]
    share = part_refs[0].shape[1]
    total = None
    for s, part_ref in enumerate(part_refs):
        start = pl.multiple_of(from_ref[s] * share, share)
        term = jnp.dot(
            part_ref[...], masked_ref[pl.ds(start, share), :], preferred_element_type=jnp.float32
        )
        total = term if total is None else total + term
    for t, out_ref in enumerate(out_refs):

        @pl.when(pl.program_id(0) == t)
        def _():
            out_ref[...] = total.astype(out_ref.dtype)


def ladder_product(came_from, goes_to, parts, masked):
    depth = len(parts)
    rows, share = parts[0].shape
    whole_pairs = masked.shape[0]
    return pl.pallas_call(
        functools.partial(ladder_kernel, depth),
        grid_spec=pltpu.PrefetchScalarGridSpec(
            num_scalar_prefetch=2,
            grid=(depth,),
            in_specs=[pl.BlockSpec((rows, share), lambda t, came, goes: (0, 0))] * depth
            + [pl.BlockSpec((whole_pairs, share), lambda t, came, goes: (0, goes[t]))],
            out_specs=[pl.BlockSpec((rows, share), lambda t, came, goes: (0, 0))] * depth,
        ),
        out_shape=[jax.ShapeDtypeStruct((rows, share), jnp.bfloat16)] * depth,
        compiler_params=pltpu.CompilerParams(vmem_limit_bytes=24 * 1024 * 1024),
        cost_estimate=pl.CostEstimate(
            flops=2 * rows * whole_pairs * whole_pairs,
            bytes_accessed=2 * whole_pairs * whole_pairs + 4 * depth * rows * share,
            transcendentals=0,
        ),
        name="ladder",
    )(came_from, goes_to, *parts, masked)


def shift(block, depth, step):
    return lax.ppermute(block, "depth", [(d, (d + step) % depth) for d in range(depth)])


def on_device(amplitudes, integrals, pair_irreps, occ_fock):
    local_i, local_j, share = amplitudes.shape
    whole_pairs = integrals.shape[0]
    whole_i = occ_fock.shape[0]
    rows = whole_i // local_i
    depth = whole_pairs // share
    hub_j = local_j // rows
    part_j = local_j // depth
    here = lax.axis_index("depth")
    steps = jnp.arange(depth, dtype=jnp.int32)
    came_from = (here - steps + depth) % depth
    goes_to = (here + steps) % depth

    blocks = amplitudes.reshape(local_i, rows, hub_j, share).transpose(1, 0, 2, 3)
    arrived = lax.all_to_all(blocks, "row", split_axis=0, concat_axis=0)

    parts = []
    for s in range(depth):
        start = ((here + s) % depth) * part_j
        part = lax.dynamic_slice(amplitudes, (0, start, 0), (local_i, part_j, share))
        parts.append(part if s == 0 else shift(part, depth, s))
    same = pair_irreps[:, None] == pair_irreps[None, :]
    masked = jnp.where(same, integrals, jnp.zeros_like(integrals))
    columns = ladder_product(
        came_from, goes_to, [part.reshape(local_i * part_j, share) for part in parts], masked
    )
    ladder = jnp.zeros_like(amplitudes)
    for t in range(depth):
        piece = columns[t].reshape(local_i, part_j, share)
        piece = piece if t == 0 else shift(piece, depth, t)
        start = ((here - t + depth) % depth) * part_j
        ladder = lax.dynamic_update_slice(ladder, piece, (0, start, 0))

    tied_fock, _ = lax.optimization_barrier((occ_fock, columns[0]))
    product = jnp.einsum(
        "ik,kmn->imn",
        tied_fock,
        arrived.reshape(whole_i, hub_j, share),
        preferred_element_type=jnp.float32,
    )
    dressed_part = (-product).astype(jnp.bfloat16).reshape(rows, local_i, hub_j, share)
    dressed = lax.all_to_all(dressed_part, "row", split_axis=0, concat_axis=0)
    dressed = dressed.transpose(1, 0, 2, 3).reshape(local_i, local_j, share)
    return (ladder.astype(jnp.float32) + dressed.astype(jnp.float32)).astype(jnp.bfloat16)


def solution(mesh):
    placed = (P("row", "col", "depth"), P(), P(), P())
    return jax.shard_map(
        on_device, mesh=mesh, in_specs=placed, out_specs=P("row", "col", "depth"), check_vma=False
    )
```
